256 devices in a mesh: dp: 8 (over y_lo, x), seq: 32 (over y_hi, z, core).
Axes of the slice: x: 4, y: 4 (y_hi: 2, y_lo: 2; y = y_hi * 2 + y_lo), z: 8, core: 2. Of those that a mesh axis runs over, the one named last changes fastest.
Arguments:
- queries: bfloat16 [65536, 4096], P(('dp', 'seq')), parts along dimension 0, may hold values from -6 to 6
- keys: bfloat16 [65536, 512], P(('dp', 'seq')), parts along dimension 0, may hold values from -6 to 6
- values: bfloat16 [65536, 512], P(('dp', 'seq')), parts along dimension 0, may hold values from -6 to 6
- doc_ids: int32 [65536], P(('dp', 'seq')), parts along dimension 0, may hold values from 0 to 15, never falling along the last dimension, each value on 1 to 4096 neighbouring positions
Outputs:
- attended: float32 [65536, 4096], P(('dp', 'seq')), parts along dimension 0
- log_total: float32 [32, 65536], P(None, ('dp', 'seq')), parts along dimension 1
The draws below stay inside these ranges and needn't reach their ends.
There are 8 independent parts, one for each index of `dp`. The reference program is written for one: setup_inputs(seed, part) draws one part's arguments, and reference() takes and returns one part's arrays. A program takes and returns all parts, laid end to end along the dimension named above; each array names one. Nothing has to cross between parts.
Inputs may be any that keep to these rules, and one draw needn't show every extreme that they name: `doc_ids`: ids never fall along positions; each document has 1 to 4096 positions and one has exactly 4096.
All inputs are finite; a program needn't handle non-finite values.
Results may differ from the reference program's by a relative error of at most 0.0017.
Values may be sent and summed in bfloat16 or wider, within the bound.
No kernel may reach another device: no remote copies, remote signals or barrier semaphores. Data moves between devices by JAX's collectives and lax.ppermute only.
A program may use at most 128 MiB of HBM per device.

```python
import math
import jax
import jax.numpy as jnp
import numpy as np
from jax import lax

QUERY_HEADS = 32
KEY_VALUE_HEADS = 4
HEAD_SIZE = 128
TOK_DEV = 256
PACKED_TOKENS = 8192
STRETCH = 128
MOST = 4096
SEGS = 16
N_SEQ = 32


def draw_queries(key, part):
    self_rows = jax.random.fold_in(key, 3)
    attention_output = jnp.clip(jax.random.normal(self_rows, (PACKED_TOKENS, QUERY_HEADS, HEAD_SIZE)), -4.0, 4.0)
    return attention_output.reshape(PACKED_TOKENS, QUERY_HEADS * HEAD_SIZE).astype(jnp.float32).astype(jnp.bfloat16)


def draw_keys(key, part):
    self_rows = jax.random.fold_in(key, 5)
    attention_output = jnp.clip(jax.random.normal(self_rows, (PACKED_TOKENS, KEY_VALUE_HEADS, HEAD_SIZE)), -4.0, 4.0)
    return attention_output.reshape(PACKED_TOKENS, KEY_VALUE_HEADS * HEAD_SIZE).astype(jnp.float32).astype(jnp.bfloat16)


def draw_values(key, part):
    noise_key, offset_key = jax.random.split(jax.random.fold_in(key, 17))
    blocks = PACKED_TOKENS // STRETCH
    columns = KEY_VALUE_HEADS * HEAD_SIZE
    noise = 0.8 * jnp.clip(jax.random.normal(noise_key, (blocks, STRETCH, columns)), -3.0, 3.0)
    level = jnp.where(jax.random.uniform(offset_key, (blocks, 1, columns)) < 0.5, 1.2, -1.2)
    return (level + noise).reshape(PACKED_TOKENS, columns).astype(jnp.float32).astype(jnp.bfloat16)


def profile(amount, total, bound, skew):
    loads = [(1 << 20) // math.isqrt(rank ** skew) + 1 for rank in range(2, amount + 1)]
    spare, counts = total - bound - (amount - 1), [1] * (amount - 1)
    while spare > 0:
        candidates = [i for i in range(amount - 1) if counts[i] < bound]
        whole, budget = sum([loads[i] for i in candidates]), spare
        for i in candidates:
            addition = min(bound - counts[i], max(1, budget * loads[i] // whole), spare)
            counts[i] = counts[i] + addition
            spare = spare - addition
    return np.array([bound] + counts)


def uneven(key, number_of, total, most, skew):
    if number_of == 2:
        one = jax.random.randint(key, (), max(1, total - most), min(most, total - 1) + 1)
        return jnp.stack([one, total - one])
    sizes = jnp.asarray(profile(number_of, total, most, skew), jnp.int32)
    pairs = (number_of - 1) // 2
    giver, taker = sizes[1:1 + 2 * pairs:2], sizes[2:2 + 2 * pairs:2]
    room = jnp.minimum(giver - 1, most - taker)
    passed = jax.random.randint(jax.random.fold_in(key, 1), (pairs,), 0, 1 << 20) % (room + 1)
    sizes = sizes.at[1:1 + 2 * pairs:2].set(giver - passed).at[2:2 + 2 * pairs:2].set(taker + passed)
    return sizes[jax.random.permutation(jax.random.fold_in(key, 2), number_of)]


def setup_inputs(seed: int = 0, part: int = 0) -> dict:
    seeds = jax.random.split(jax.random.key(seed), 5)
    own_keys = jax.random.split(jax.random.fold_in(seeds[4], part), 5)
    queries = draw_queries(jax.random.fold_in(jax.random.fold_in(seeds[4], part), 71), part)
    keys = draw_keys(jax.random.fold_in(jax.random.fold_in(seeds[4], part), 71), part)
    values = draw_values(jax.random.fold_in(jax.random.fold_in(seeds[4], part), 71), part)
    doc_ids = jnp.searchsorted(jnp.cumsum(uneven(own_keys[3], SEGS, PACKED_TOKENS, MOST, 2)), jnp.arange(PACKED_TOKENS), side="right").astype(jnp.int32)
    return {"queries": queries, "keys": keys, "values": values, "doc_ids": doc_ids}


def stored_to_stretch(count):
    order = jnp.arange(count, dtype=jnp.int32)
    pair = order // 2
    return jnp.where(order % 2 == 0, pair, count - 1 - pair)


def reference(queries, keys, values, doc_ids):
    half_span = TOK_DEV // 2
    count = 2 * N_SEQ
    head_group = QUERY_HEADS // KEY_VALUE_HEADS
    natural = jnp.arange(count, dtype=jnp.int32)
    source = jnp.where(natural < N_SEQ, 2 * natural, 2 * (count - 1 - natural) + 1)

    def reorder(array):
        return array.reshape(count, half_span, -1)[source].reshape(PACKED_TOKENS, -1)

    query_natural = reorder(queries)
    key_natural = jnp.pad(reorder(keys), ((MOST, 0), (0, 0)))
    value_natural = jnp.pad(reorder(values), ((MOST, 0), (0, 0)))
    doc_pad = jnp.pad(doc_ids, (MOST, 0), constant_values=-1)
    token_span = MOST + half_span
    scale = 1.0 / (HEAD_SIZE ** 0.5)

    def one_block(block):
        leading_part = (block * half_span).astype(jnp.int32)
        query_block = lax.dynamic_slice_in_dim(query_natural, leading_part, half_span).astype(jnp.float32).reshape(half_span, KEY_VALUE_HEADS, head_group, HEAD_SIZE)
        key_block = lax.dynamic_slice_in_dim(key_natural, leading_part, token_span).astype(jnp.float32).reshape(token_span, KEY_VALUE_HEADS, HEAD_SIZE)
        value_block = lax.dynamic_slice_in_dim(value_natural, leading_part, token_span).astype(jnp.float32).reshape(token_span, KEY_VALUE_HEADS, HEAD_SIZE)
        key_doc = lax.dynamic_slice_in_dim(doc_pad, leading_part, token_span)
        query_doc = lax.dynamic_slice_in_dim(doc_pad, leading_part + MOST, half_span)
        query_pos = leading_part + jnp.arange(half_span, dtype=jnp.int32)
        key_pos = leading_part - MOST + jnp.arange(token_span, dtype=jnp.int32)
        visible = (query_doc[:, None] == key_doc[None, :]) & (key_pos[None, :] <= query_pos[:, None])
        scores = jnp.einsum("qhgd,khd->hgqk", query_block, key_block, precision=lax.Precision.HIGHEST) * scale
        top = jnp.max(jnp.where(visible, scores, -jnp.inf), axis=-1)
        weights = jnp.where(visible, jnp.exp(scores - top[..., None]), 0.0)
        total = jnp.sum(weights, axis=-1)
        rounded = lax.optimization_barrier(weights.astype(jnp.bfloat16)).astype(jnp.float32)
        mixed = jnp.einsum("hgqk,khd->qhgd", rounded, value_block, precision=lax.Precision.HIGHEST)
        mixed = mixed / jnp.transpose(total, (2, 0, 1))[..., None]
        attention_output = mixed.reshape(half_span, QUERY_HEADS * HEAD_SIZE)
        return attention_output, (top + jnp.log(total)).reshape(QUERY_HEADS, half_span)

    outputs, sums = lax.map(one_block, jnp.arange(count, dtype=jnp.int32))
    stretch_of = stored_to_stretch(count)
    attended = outputs[stretch_of].reshape(PACKED_TOKENS, QUERY_HEADS * HEAD_SIZE)
    log_total = jnp.transpose(sums[stretch_of], (1, 0, 2)).reshape(QUERY_HEADS, PACKED_TOKENS)
    return attended, log_total
```

```python
import functools
import math

import jax
import jax.numpy as jnp
from jax import lax
from jax.experimental import pallas as pl
from jax.experimental.pallas import tpu as pltpu
from jax.sharding import Mesh
from jax.sharding import PartitionSpec as P

HEAD = 128
ST = 128
DOCS = 16
PACKED = 8192
SCALE = 1.0 / math.sqrt(HEAD)
SCALE2 = SCALE * math.log2(math.e)
LOW = -1e30
AXES = ("ylo", "x", "yhi", "z", "core")
SEQ = ("yhi", "z", "core")
RATIO = 8
SIDE = 4


def attend_kernel(pieces, arrays, *refs):
    meta, starts, queries = refs[:3]
    blocks = refs[3 : 3 + arrays]
    out, logs = refs[3 + arrays : 5 + arrays]
    buf, sems, todo, edge, plan, bias, doc_q, doc_k, ext, state, done, out_sems = refs[5 + arrays :]
    me = meta[0]
    n_pieces = len(pieces)

    def start_of(pos):
        best = jnp.int32(0)
        for d in range(DOCS):
            best = jnp.where(starts[d] <= pos, jnp.maximum(best, starts[d]), best)
        return best

    rows = lax.broadcasted_iota(jnp.int32, (ST, ST), 0)
    lane = lax.broadcasted_iota(jnp.int32, (ST, HEAD), 1)
    opens = closes = jnp.zeros((ST, HEAD), jnp.int32)
    for d in range(DOCS):
        opens = jnp.where(lane == d, starts[d], opens)
        closes = jnp.where(lane == d, starts[d + 1] if d + 1 < DOCS else PACKED, closes)

    total, steps = jnp.int32(0), jnp.int32(0)
    ends = []
    for w in range(2):
        stretch = me if w == 0 else 63 - me
        pos = stretch * ST + rows
        doc_q[w] = jnp.where((pos >= opens) & (pos < closes), 1.0, 0.0).astype(jnp.bfloat16)
        lowest = start_of(stretch * ST)

        def consider(i, counts, stretch=stretch, lowest=lowest):
            whole, part = counts
            piece = i // 2
            half = i % 2
            chip = meta[1 + 2 * piece]
            lo = jnp.where(half == 0, 2 * chip, 62 - 2 * chip)
            needed = (lo <= stretch) & ((lo + 2) * ST > lowest)
            clear = needed & (lo + 1 < stretch)

            @pl.when(clear)
            def _():
                todo[0, whole] = i
                todo[1, whole] = lo * ST

            @pl.when(needed & ~clear)
            def _():
                edge[0, part] = i
                edge[1, part] = lo * ST

            clear = clear.astype(jnp.int32)
            return whole + clear, part + needed.astype(jnp.int32) - clear

        whole, part = lax.fori_loop(0, 2 * n_pieces, consider, (total, jnp.int32(0)))

        def move(i, _, whole=whole):
            todo[0, whole + i] = edge[0, i]
            todo[1, whole + i] = edge[1, i]
            return 0

        lax.fori_loop(0, part, move, 0)
        many = (whole - total) // SIDE

        def together(i, _, total=total, steps=steps):
            plan[0, steps + i] = total + i * SIDE
            plan[1, steps + i] = SIDE
            return 0

        lax.fori_loop(0, many, together, 0)
        total, steps = total + many * SIDE, steps + many

        def single(i, _, total=total, steps=steps):
            plan[0, steps + i] = total + i
            plan[1, steps + i] = 1
            return 0

        rest = whole + part - total
        lax.fori_loop(0, rest, single, 0)
        total, steps = total + rest, steps + rest
        ends.append(steps)

    def fetch(group):
        slot = group % 2

        def one(u, _):
            which = todo[0, plan[0, group] + u]
            half = which % 2
            for j, piece in enumerate(pieces):

                @pl.when(which // 2 == j)
                def _():
                    for c, (array, row) in enumerate(piece):
                        pltpu.make_async_copy(
                            blocks[array].at[pl.ds(pl.multiple_of(row + half * ST, ST), ST), :],
                            buf.at[slot, pl.ds(pl.multiple_of((2 * u + c) * ST, ST), ST), :],
                            sems.at[slot, u, c],
                        ).start()

            return 0

        lax.fori_loop(0, plan[1, group], one, 0)

    def arrived(group):
        slot = group % 2

        def one(u, _):
            for c in range(2):
                pltpu.make_async_copy(
                    blocks[0].at[pl.ds(0, ST), :],
                    buf.at[slot, pl.ds(pl.multiple_of((2 * u + c) * ST, ST), ST), :],
                    sems.at[slot, u, c],
                ).wait()
            return 0

        lax.fori_loop(0, plan[1, group], one, 0)

    def fold(group, masked):
        slot, w = group % 2, jnp.where(group < ends[0], 0, 1)
        wide = 2 * ST if masked else SIDE * 2 * ST
        here = pl.ds(pl.multiple_of(w * ST, ST), ST)
        for g in range(4):
            ext[g, 0:wide, 0:HEAD] = buf[slot, 0:wide, 512 + g * HEAD : 512 + (g + 1) * HEAD]
            key = jnp.concatenate(
                [buf[slot, 0:wide, g * HEAD : (g + 1) * HEAD], doc_k[0:wide, :]], axis=1
            )
            base = g * RATIO
            query = jnp.concatenate(
                [
                    jnp.concatenate(
                        [queries[here, (base + e) * HEAD : (base + e + 1) * HEAD], doc_q[w]], axis=1
                    )
                    for e in range(RATIO)
                ],
                axis=0,
            )
            scores = lax.dot_general(
                query, key, (((1,), (1,)), ((), ())), preferred_element_type=jnp.float32
            )
            if masked:
                scores = (scores.reshape(RATIO, ST, wide) + bias[...][None]).reshape(
                    RATIO * ST, wide
                )
            held = state[base : base + RATIO].reshape(RATIO * ST, 3 * HEAD)
            prior = held[:, 2 * HEAD :]
            top = jnp.maximum(prior, jnp.max(scores, axis=1, keepdims=True))
            spread = jnp.concatenate([top] * (wide // HEAD), axis=1)
            weights = jnp.exp2((scores - spread) * SCALE2).astype(jnp.bfloat16)
            mixed = jnp.dot(weights, ext[g, 0:wide], preferred_element_type=jnp.float32)
            fade = jnp.exp2((prior - top) * SCALE2)
            sums = held[:, : 2 * HEAD] * jnp.concatenate([fade, fade], axis=1) + mixed
            state[base : base + RATIO, :, 0 : 2 * HEAD] = sums.reshape(RATIO, ST, 2 * HEAD)
            state[base : base + RATIO, :, 2 * HEAD :] = top.reshape(RATIO, ST, HEAD)

    def shift_of(which, c):
        swapped = (which + meta[2 + 2 * (which // 2)]) % 2
        return jnp.where(swapped == 0, c, 1 - c) * ST

    def label(group):
        def one(u, _):
            entry = plan[0, group] + u
            for c in range(2):
                pos = todo[1, entry] + shift_of(todo[0, entry], c) + rows
                mine = (pos >= opens) & (pos < closes)
                doc_k[pl.ds(pl.multiple_of((2 * u + c) * ST, ST), ST), :] = jnp.where(
                    mine, 0.0, LOW
                ).astype(jnp.bfloat16)
            return 0

        lax.fori_loop(0, plan[1, group], one, 0)

    def mask(group):
        pos = jnp.where(group < ends[0], me, 63 - me) * ST + rows
        entry = plan[0, group]
        for c in range(2):
            key_pos = todo[1, entry] + shift_of(todo[0, entry], c) + lane
            bias[:, c * ST : (c + 1) * ST] = jnp.where(key_pos <= pos, 0.0, LOW)

    def send(w, g):
        return pltpu.make_async_copy(
            done.at[w, :, pl.ds(g * 1024, 1024)],
            out.at[pl.ds(w * ST, ST), pl.ds(g * 1024, 1024)],
            out_sems.at[w, g],
        )

    fetch(0)
    for g in range(4):
        ext[g, :, HEAD:] = jnp.ones((SIDE * 2 * ST, HEAD), jnp.bfloat16)

    def clean(h, _):
        state[h, :, 0 : 2 * HEAD] = jnp.zeros((ST, 2 * HEAD), jnp.float32)
        state[h, :, 2 * HEAD :] = jnp.full((ST, HEAD), LOW, jnp.float32)
        return 0

    def finish(w):
        totals = jnp.ones((ST, HEAD), jnp.float32)
        tops = jnp.zeros((ST, HEAD), jnp.float32)
        for g in range(4):
            for h in range(8 * g, 8 * g + 8):
                weight = state[h, :, HEAD : 2 * HEAD]
                done[w, :, h * HEAD : (h + 1) * HEAD] = state[h, :, 0:HEAD] / weight
                totals = jnp.where(lane == h, weight, totals)
                tops = jnp.where(lane == h, state[h, :, 2 * HEAD :], tops)
            send(w, g).start()
        logs[:, w * ST : (w + 1) * ST] = (tops * SCALE + jnp.log(totals)).T[0:32]

    lax.fori_loop(0, 32, clean, 0)

    def step(group, _):
        @pl.when(group + 1 < ends[1])
        def _():
            fetch(group + 1)

        label(group)
        arrived(group)

        @pl.when(plan[1, group] == 1)
        def _():
            mask(group)
            fold(group, True)

        @pl.when(plan[1, group] == SIDE)
        def _():
            fold(group, False)

        @pl.when(group + 1 == ends[0])
        def _():
            finish(0)
            lax.fori_loop(0, 32, clean, 0)

        return 0

    lax.fori_loop(0, ends[1], step, 0)
    finish(1)
    for w in range(2):
        for g in range(4):
            send(w, g).wait()


def attend(meta, starts, queries, pieces):
    arrays, index, static = [], {}, []

    def place(block):
        array, row = block
        if id(array) not in index:
            index[id(array)] = len(arrays)
            arrays.append(array)
        return (index[id(array)], row)

    for piece in pieces:
        static.append(tuple(place(block) for block in piece))
    smem = pl.BlockSpec(memory_space=pltpu.SMEM)
    vmem = pl.BlockSpec(memory_space=pltpu.VMEM)
    hbm = pl.BlockSpec(memory_space=pltpu.HBM)
    wide = SIDE * 2 * ST
    return pl.pallas_call(
        functools.partial(attend_kernel, tuple(static), len(arrays)),
        out_shape=(
            jax.ShapeDtypeStruct((2 * ST, 32 * HEAD), jnp.float32),
            jax.ShapeDtypeStruct((32, 2 * ST), jnp.float32),
        ),
        in_specs=[smem, smem, vmem] + [hbm] * len(arrays),
        out_specs=(hbm, vmem),
        scratch_shapes=[
            pltpu.VMEM((2, wide, 1024), jnp.bfloat16),
            pltpu.SemaphoreType.DMA((2, SIDE, 2)),
            pltpu.SMEM((2, 4 * len(static)), jnp.int32),
            pltpu.SMEM((2, 2 * len(static)), jnp.int32),
            pltpu.SMEM((2, 4 * len(static)), jnp.int32),
            pltpu.VMEM((ST, 2 * ST), jnp.float32),
            pltpu.VMEM((2, ST, HEAD), jnp.bfloat16),
            pltpu.VMEM((wide, HEAD), jnp.bfloat16),
            pltpu.VMEM((4, wide, 2 * HEAD), jnp.bfloat16),
            pltpu.VMEM((32, ST, 3 * HEAD), jnp.float32),
            pltpu.VMEM((2, ST, 32 * HEAD), jnp.float32),
            pltpu.SemaphoreType.DMA((2, 4)),
        ],
        compiler_params=pltpu.CompilerParams(vmem_limit_bytes=56 * 2**20),
        cost_estimate=pl.CostEstimate(
            flops=20 * 10**9, bytes_accessed=10**7, transcendentals=0
        ),
    )(meta, starts, queries, *arrays)


def on_device(queries, keys, values, doc_ids):
    yhi, z, core = (lax.axis_index(a) for a in SEQ)
    me = (yhi * 8 + z) * 2 + core
    n_z = 8

    def swap(x):
        return lax.ppermute(x, "core", [(0, 1), (1, 0)])

    def across(x):
        return lax.ppermute(x, "yhi", [(0, 1), (1, 0)])

    def along(x):
        pairs = []
        for i in range(n_z):
            pairs.append((2 * i, 2 * ((i + 1) % n_z)))
            pairs.append((2 * i + 1, 2 * ((i - 1) % n_z) + 1))
        return lax.ppermute(x, ("z", "core"), pairs)

    below = jnp.sum(
        (doc_ids[None, :] < jnp.arange(DOCS, dtype=jnp.int32)[:, None]).astype(jnp.float32), axis=1
    )
    extra = jnp.pad(below.astype(jnp.bfloat16)[None, :], ((0, 15), (0, 1024 - DOCS)))
    own = jnp.concatenate([jnp.concatenate([keys, values], 1), extra], 0)
    side = swap(own)
    over = across(own)
    over_side = swap(over)

    def chip(y_off, z_off):
        return ((yhi + y_off) % 2) * 8 + (z + z_off) % n_z

    back = jnp.where(core == 0, -1, 1)
    pieces = [[(own, 0), (side, 0)], [(over, 0), (over_side, 0)]]
    entries = [(chip(0, 0), core), (chip(1, 0), core)]
    counts = [x[256] for x in (own, side, over, over_side)]

    def ring(x, y_off, d):
        other = swap(x)
        pieces.extend([[(x, 0), (x, 256)], [(other, 0), (other, 256)]])
        entries.extend([(chip(y_off, d * back), 0), (chip(y_off, -d * back), 0)])
        counts.extend([x[512], x[513], other[512], other[513]])

    def opposite(x, y_off):
        pieces.append([(x, 0), (swap(x), 0)])
        entries.append((chip(y_off, 4), core))
        counts.extend([x[256], x[257]])

    def half(x):
        return jnp.concatenate([jnp.where(core == 0, x[:256], x[256:512]), x[512:528]], 0)

    def joined(mine, other):
        first, second = jnp.where(core == 0, mine, other), jnp.where(core == 0, other, mine)
        return jnp.concatenate([first[:256], second[:256], first[256:257], second[256:271]], 0)

    p1 = along(joined(own, side))
    q1 = along(joined(over, over_side))
    p2 = along(p1)
    q2 = across(p2)
    p3 = along(p2)
    p4 = along(half(p3))
    q4 = across(p4)
    q3 = along(q2)
    ring(p1, 0, 1)
    ring(p2, 0, 2)
    ring(q1, 1, 1)
    ring(p3, 0, 3)
    ring(q2, 1, 2)
    opposite(p4, 0)
    ring(q3, 1, 3)
    opposite(q4, 1)
    starts = sum(x[:DOCS].astype(jnp.float32) for x in counts).astype(jnp.int32)
    flat = [me]
    for c, lead in entries:
        flat += [c, lead]
    meta = jnp.stack([jnp.asarray(v, jnp.int32) for v in flat])
    return attend(meta, starts, queries, pieces)


def solution(mesh):
    split = Mesh(mesh.devices.reshape(2, 4, 2, 8, 2), AXES)
    return jax.shard_map(
        on_device,
        mesh=split,
        in_specs=(P(AXES, None), P(AXES, None), P(AXES, None), P(AXES)),
        out_specs=(P(AXES, None), P(None, AXES)),
        check_vma=False,
    )
```

```python
import functools
import math

import jax
import jax.numpy as jnp
from jax import lax
from jax.experimental import pallas as pl
from jax.experimental.pallas import tpu as pltpu
from jax.sharding import Mesh
from jax.sharding import PartitionSpec as P

HEAD = 128
ST = 128
DOCS = 16
PACKED = 8192
SCALE = 1.0 / math.sqrt(HEAD)
SCALE2 = SCALE * math.log2(math.e)
LOW = -1e30
AXES = ("ylo", "x", "yhi", "z", "core")
SEQ = ("yhi", "z", "core")
RATIO = 8
SIDE = 4


def attend_kernel(pieces, arrays, *refs):
    meta, starts, queries = refs[:3]
    blocks = refs[3 : 3 + arrays]
    out, logs = refs[3 + arrays : 5 + arrays]
    buf, sems, todo, edge, plan, bias, doc_q, doc_k, state, done, out_sems = refs[5 + arrays :]
    me = meta[0]
    n_pieces = len(pieces)

    def start_of(pos):
        best = jnp.int32(0)
        for d in range(DOCS):
            best = jnp.where(starts[d] <= pos, jnp.maximum(best, starts[d]), best)
        return best

    rows = lax.broadcasted_iota(jnp.int32, (ST, ST), 0)
    lane = lax.broadcasted_iota(jnp.int32, (ST, HEAD), 1)
    opens = closes = jnp.zeros((ST, HEAD), jnp.int32)
    for d in range(DOCS):
        opens = jnp.where(lane == d, starts[d], opens)
        closes = jnp.where(lane == d, starts[d + 1] if d + 1 < DOCS else PACKED, closes)

    total, steps = jnp.int32(0), jnp.int32(0)
    ends = []
    for w in range(2):
        stretch = me if w == 0 else 63 - me
        pos = stretch * ST + rows
        doc_q[w] = jnp.where((pos >= opens) & (pos < closes), 1.0, 0.0).astype(jnp.bfloat16)
        lowest = start_of(stretch * ST)

        def consider(i, counts, stretch=stretch, lowest=lowest):
            whole, part = counts
            piece = i // 2
            half = i % 2
            chip = meta[1 + 2 * piece]
            lo = jnp.where(half == 0, 2 * chip, 62 - 2 * chip)
            needed = (lo <= stretch) & ((lo + 2) * ST > lowest)
            clear = needed & (lo + 1 < stretch)

            @pl.when(clear)
            def _():
                todo[0, whole] = i
                todo[1, whole] = lo * ST

            @pl.when(needed & ~clear)
            def _():
                edge[0, part] = i
                edge[1, part] = lo * ST

            clear = clear.astype(jnp.int32)
            return whole + clear, part + needed.astype(jnp.int32) - clear

        whole, part = lax.fori_loop(0, 2 * n_pieces, consider, (total, jnp.int32(0)))

        def move(i, _, whole=whole):
            todo[0, whole + i] = edge[0, i]
            todo[1, whole + i] = edge[1, i]
            return 0

        lax.fori_loop(0, part, move, 0)
        many = (whole - total) // SIDE

        def together(i, _, total=total, steps=steps):
            plan[0, steps + i] = total + i * SIDE
            plan[1, steps + i] = SIDE
            return 0

        lax.fori_loop(0, many, together, 0)
        total, steps = total + many * SIDE, steps + many

        def single(i, _, total=total, steps=steps):
            plan[0, steps + i] = total + i
            plan[1, steps + i] = 1
            return 0

        rest = whole + part - total
        lax.fori_loop(0, rest, single, 0)
        total, steps = total + rest, steps + rest
        ends.append(steps)

    def fetch(group):
        slot = group % 2

        def one(u, _):
            which = todo[0, plan[0, group] + u]
            half = which % 2
            for j, piece in enumerate(pieces):

                @pl.when(which // 2 == j)
                def _():
                    for c, (array, row) in enumerate(piece):
                        pltpu.make_async_copy(
                            blocks[array].at[pl.ds(pl.multiple_of(row + half * ST, ST), ST), :],
                            buf.at[slot, pl.ds(pl.multiple_of((2 * u + c) * ST, ST), ST), :],
                            sems.at[slot, u, c],
                        ).start()

            return 0

        lax.fori_loop(0, plan[1, group], one, 0)

    def arrived(group):
        slot = group % 2

        def one(u, _):
            for c in range(2):
                pltpu.make_async_copy(
                    blocks[0].at[pl.ds(0, ST), :],
                    buf.at[slot, pl.ds(pl.multiple_of((2 * u + c) * ST, ST), ST), :],
                    sems.at[slot, u, c],
                ).wait()
            return 0

        lax.fori_loop(0, plan[1, group], one, 0)

    def fold(group, masked):
        slot, w = group % 2, jnp.where(group < ends[0], 0, 1)
        wide = 2 * ST if masked else SIDE * 2 * ST
        here = pl.ds(pl.multiple_of(w * ST, ST), ST)
        for g in range(4):
            value = buf[slot, 0:wide, 512 + g * HEAD : 512 + (g + 1) * HEAD]
            key = jnp.concatenate(
                [buf[slot, 0:wide, g * HEAD : (g + 1) * HEAD], doc_k[0:wide, :]], axis=1
            )
            base = g * RATIO
            query = jnp.concatenate(
                [
                    jnp.concatenate(
                        [queries[here, (base + e) * HEAD : (base + e + 1) * HEAD], doc_q[w]], axis=1
                    )
                    for e in range(RATIO)
                ],
                axis=0,
            )
            scores = lax.dot_general(
                query, key, (((1,), (1,)), ((), ())), preferred_element_type=jnp.float32
            )
            if masked:
                scores = (scores.reshape(RATIO, ST, wide) + bias[...][None]).reshape(
                    RATIO * ST, wide
                )
            held = state[base : base + RATIO].reshape(RATIO * ST, 3 * HEAD)
            prior = held[:, 2 * HEAD :]
            top = jnp.maximum(prior, jnp.max(scores, axis=1, keepdims=True))
            spread = jnp.concatenate([top] * (wide // HEAD), axis=1)
            weights = jnp.exp2((scores - spread) * SCALE2)
            mixed = jnp.dot(
                weights.astype(jnp.bfloat16), value, preferred_element_type=jnp.float32
            )
            part = sum(weights[:, t * HEAD : (t + 1) * HEAD] for t in range(wide // HEAD))
            fade = jnp.exp2((prior - top) * SCALE2)
            sums = jnp.concatenate(
                [held[:, :HEAD] * fade + mixed, held[:, HEAD : 2 * HEAD] * fade + part], axis=1
            )
            state[base : base + RATIO, :, 0 : 2 * HEAD] = sums.reshape(RATIO, ST, 2 * HEAD)
            state[base : base + RATIO, :, 2 * HEAD :] = top.reshape(RATIO, ST, HEAD)

    def shift_of(which, c):
        swapped = (which + meta[2 + 2 * (which // 2)]) % 2
        return jnp.where(swapped == 0, c, 1 - c) * ST

    def label(group):
        def one(u, _):
            entry = plan[0, group] + u
            for c in range(2):
                pos = todo[1, entry] + shift_of(todo[0, entry], c) + rows
                mine = (pos >= opens) & (pos < closes)
                doc_k[pl.ds(pl.multiple_of((2 * u + c) * ST, ST), ST), :] = jnp.where(
                    mine, 0.0, LOW
                ).astype(jnp.bfloat16)
            return 0

        lax.fori_loop(0, plan[1, group], one, 0)

    def mask(group):
        pos = jnp.where(group < ends[0], me, 63 - me) * ST + rows
        entry = plan[0, group]
        for c in range(2):
            key_pos = todo[1, entry] + shift_of(todo[0, entry], c) + lane
            bias[:, c * ST : (c + 1) * ST] = jnp.where(key_pos <= pos, 0.0, LOW)

    def send(w, g):
        return pltpu.make_async_copy(
            done.at[w, :, pl.ds(g * 1024, 1024)],
            out.at[pl.ds(w * ST, ST), pl.ds(g * 1024, 1024)],
            out_sems.at[w, g],
        )

    fetch(0)

    def clean(h, _):
        state[h, :, 0 : 2 * HEAD] = jnp.zeros((ST, 2 * HEAD), jnp.float32)
        state[h, :, 2 * HEAD :] = jnp.full((ST, HEAD), LOW, jnp.float32)
        return 0

    def finish(w):
        totals = jnp.ones((ST, HEAD), jnp.float32)
        tops = jnp.zeros((ST, HEAD), jnp.float32)
        for g in range(4):
            for h in range(8 * g, 8 * g + 8):
                weight = jnp.sum(state[h, :, HEAD : 2 * HEAD], axis=1, keepdims=True)
                done[w, :, h * HEAD : (h + 1) * HEAD] = state[h, :, 0:HEAD] / weight
                totals = jnp.where(lane == h, weight, totals)
                tops = jnp.where(lane == h, state[h, :, 2 * HEAD :], tops)
            send(w, g).start()
        logs[:, w * ST : (w + 1) * ST] = (tops * SCALE + jnp.log(totals)).T[0:32]

    lax.fori_loop(0, 32, clean, 0)

    def step(group, _):
        @pl.when(group + 1 < ends[1])
        def _():
            fetch(group + 1)

        label(group)
        arrived(group)

        @pl.when(plan[1, group] == 1)
        def _():
            mask(group)
            fold(group, True)

        @pl.when(plan[1, group] == SIDE)
        def _():
            fold(group, False)

        @pl.when(group + 1 == ends[0])
        def _():
            finish(0)
            lax.fori_loop(0, 32, clean, 0)

        return 0

    lax.fori_loop(0, ends[1], step, 0)
    finish(1)
    for w in range(2):
        for g in range(4):
            send(w, g).wait()


def attend(meta, starts, queries, pieces):
    arrays, index, static = [], {}, []

    def place(block):
        array, row = block
        if id(array) not in index:
            index[id(array)] = len(arrays)
            arrays.append(array)
        return (index[id(array)], row)

    for piece in pieces:
        static.append(tuple(place(block) for block in piece))
    smem = pl.BlockSpec(memory_space=pltpu.SMEM)
    vmem = pl.BlockSpec(memory_space=pltpu.VMEM)
    hbm = pl.BlockSpec(memory_space=pltpu.HBM)
    wide = SIDE * 2 * ST
    return pl.pallas_call(
        functools.partial(attend_kernel, tuple(static), len(arrays)),
        out_shape=(
            jax.ShapeDtypeStruct((2 * ST, 32 * HEAD), jnp.float32),
            jax.ShapeDtypeStruct((32, 2 * ST), jnp.float32),
        ),
        in_specs=[smem, smem, vmem] + [hbm] * len(arrays),
        out_specs=(hbm, vmem),
        scratch_shapes=[
            pltpu.VMEM((2, wide, 1024), jnp.bfloat16),
            pltpu.SemaphoreType.DMA((2, SIDE, 2)),
            pltpu.SMEM((2, 4 * len(static)), jnp.int32),
            pltpu.SMEM((2, 2 * len(static)), jnp.int32),
            pltpu.SMEM((2, 4 * len(static)), jnp.int32),
            pltpu.VMEM((ST, 2 * ST), jnp.float32),
            pltpu.VMEM((2, ST, HEAD), jnp.bfloat16),
            pltpu.VMEM((wide, HEAD), jnp.bfloat16),
            pltpu.VMEM((32, ST, 3 * HEAD), jnp.float32),
            pltpu.VMEM((2, ST, 32 * HEAD), jnp.float32),
            pltpu.SemaphoreType.DMA((2, 4)),
        ],
        compiler_params=pltpu.CompilerParams(vmem_limit_bytes=56 * 2**20),
        cost_estimate=pl.CostEstimate(
            flops=20 * 10**9, bytes_accessed=10**7, transcendentals=0
        ),
    )(meta, starts, queries, *arrays)


def on_device(queries, keys, values, doc_ids):
    yhi, z, core = (lax.axis_index(a) for a in SEQ)
    me = (yhi * 8 + z) * 2 + core
    n_z = 8

    def swap(x):
        return lax.ppermute(x, "core", [(0, 1), (1, 0)])

    def across(x):
        return lax.ppermute(x, "yhi", [(0, 1), (1, 0)])

    def along(x):
        pairs = []
        for i in range(n_z):
            pairs.append((2 * i, 2 * ((i + 1) % n_z)))
            pairs.append((2 * i + 1, 2 * ((i - 1) % n_z) + 1))
        return lax.ppermute(x, ("z", "core"), pairs)

    below = jnp.sum(
        (doc_ids[None, :] < jnp.arange(DOCS, dtype=jnp.int32)[:, None]).astype(jnp.float32), axis=1
    )
    extra = jnp.pad(below.astype(jnp.bfloat16)[None, :], ((0, 15), (0, 1024 - DOCS)))
    own = jnp.concatenate([jnp.concatenate([keys, values], 1), extra], 0)
    side = swap(own)
    over = across(own)
    over_side = swap(over)

    def chip(y_off, z_off):
        return ((yhi + y_off) % 2) * 8 + (z + z_off) % n_z

    back = jnp.where(core == 0, -1, 1)
    pieces = [[(own, 0), (side, 0)], [(over, 0), (over_side, 0)]]
    entries = [(chip(0, 0), core), (chip(1, 0), core)]
    counts = [x[256] for x in (own, side, over, over_side)]

    def ring(x, y_off, d):
        other = swap(x)
        pieces.extend([[(x, 0), (x, 256)], [(other, 0), (other, 256)]])
        entries.extend([(chip(y_off, d * back), 0), (chip(y_off, -d * back), 0)])
        counts.extend([x[512], x[513], other[512], other[513]])

    def opposite(x, y_off):
        pieces.append([(x, 0), (swap(x), 0)])
        entries.append((chip(y_off, 4), core))
        counts.extend([x[256], x[257]])

    def half(x):
        return jnp.concatenate([jnp.where(core == 0, x[:256], x[256:512]), x[512:528]], 0)

    def joined(mine, other):
        first, second = jnp.where(core == 0, mine, other), jnp.where(core == 0, other, mine)
        return jnp.concatenate([first[:256], second[:256], first[256:257], second[256:271]], 0)

    p1 = along(joined(own, side))
    q1 = along(joined(over, over_side))
    p2 = along(p1)
    q2 = across(p2)
    p3 = along(p2)
    p4 = along(half(p3))
    q4 = across(p4)
    q3 = along(q2)
    ring(p1, 0, 1)
    ring(p2, 0, 2)
    ring(q1, 1, 1)
    ring(p3, 0, 3)
    ring(q2, 1, 2)
    opposite(p4, 0)
    ring(q3, 1, 3)
    opposite(q4, 1)
    starts = sum(x[:DOCS].astype(jnp.float32) for x in counts).astype(jnp.int32)
    flat = [me]
    for c, lead in entries:
        flat += [c, lead]
    meta = jnp.stack([jnp.asarray(v, jnp.int32) for v in flat])
    return attend(meta, starts, queries, pieces)


def solution(mesh):
    split = Mesh(mesh.devices.reshape(2, 4, 2, 8, 2), AXES)
    return jax.shard_map(
        on_device,
        mesh=split,
        in_specs=(P(AXES, None), P(AXES, None), P(AXES, None), P(AXES)),
        out_specs=(P(AXES, None), P(None, AXES)),
        check_vma=False,
    )
```
